32 devices in a mesh: seq: 8 (over z, core), head: 4 (over y, x).
Axes of the slice: x: 2, y: 2, z: 4, core: 2. Of those that a mesh axis runs over, the one named last changes fastest.
Arguments:
- x_in: bfloat16 [8192, 8192], P('seq', 'head'), may hold values from -6 to 6
- z_gate: bfloat16 [8192, 8192], P('seq', 'head'), may hold values from -6 to 6
- b_in: bfloat16 [8192, 128], P('seq'), may hold values from -6.5 to 6.5
- c_in: bfloat16 [8192, 128], P('seq'), may hold values from -6 to 6
- dt_raw: float32 [8192, 128], P('seq', 'head'), may hold values from -7.5 to 132.072
- a_log: float32 [128], P('head'), may hold values from -12 to 3.5, as said below
- d_skip: float32 [128], P('head'), may hold values from 0.5 to 1.5
- conv_x: float32 [4, 8192], P(None, 'head'), may hold values from -3 to 3
- conv_bc: float32 [4, 256], replicated, may hold values from -0.8 to 0.8
- norm_gain: float32 [8192], P('head'), may hold values from 0.1 to 1.9
- w_out: bfloat16 [8192, 4096], P('head'), may hold values from -0.0625 to 0.0625
Outputs:
- mixed: bfloat16 [8192, 4096], P(('seq', 'head'))
The draws below stay inside these ranges and needn't reach their ends.
Inputs may be any that keep to these rules, and one draw needn't show every extreme that they name: `a_log`: logarithm of each head's decay rate.
All inputs are finite; a program needn't handle non-finite values.
Results may differ from the reference program's by a relative error of at most 0.018.
Values may be sent and summed in bfloat16 or wider, within the bound.
A program may use at most 128 MiB of HBM per device.

```python
import jax
import jax.numpy as jnp
from jax import lax

D = 4096
HEADS = 128
HEAD_DIM = 64
STATE = 128
KCONV = 4
SPAN = 256
SEQ_SPAN_LOCAL = 1024
INNER = 8192
FRAME_LENGTH = 8192
N_HEAD = 4


def head_offsets(key):
    return jax.random.uniform(jax.random.fold_in(key, 41), (HEADS,), jnp.float32, -1.2, 1.2)


def head_step_mean(key):
    return jax.nn.softplus(-4.75 + head_offsets(key))


def pulse_plan(key):
    live_key, line_key, depth_key = jax.random.split(jax.random.fold_in(key, 57), 3)
    cluster_total = FRAME_LENGTH // SEQ_SPAN_LOCAL
    pulse_live = jax.random.uniform(live_key, (cluster_total,), jnp.float32) < 0.5
    pulse_line = jnp.floor(jax.random.uniform(line_key, (cluster_total,), jnp.float32, 0.0, 0.999) * SEQ_SPAN_LOCAL)
    depth = jax.random.uniform(depth_key, (cluster_total,), jnp.float32, 0.2, 0.5)
    rows = jnp.arange(FRAME_LENGTH)
    cluster_table = rows // SEQ_SPAN_LOCAL
    inside_segment = (rows % SEQ_SPAN_LOCAL).astype(jnp.float32)
    flagged = pulse_live[cluster_table] & (inside_segment == pulse_line[cluster_table])
    return (flagged, depth[cluster_table])


def bc_taps(key):
    sign_key, size_key = jax.random.split(jax.random.fold_in(key, 31), 2)
    signs = jnp.where(jax.random.uniform(sign_key, (2 * STATE,), jnp.float32) < 0.5, -1.0, 1.0)
    sizes = jax.random.uniform(size_key, (KCONV, 2 * STATE), jnp.float32, 0.1, 0.8)
    return sizes * signs[None, :]


def draw_conv_bc(key, part):
    return bc_taps(key).astype(jnp.float32)


def draw_b_in(key, part):
    taps = bc_taps(key)[:, :STATE]
    offset = -0.5 * jnp.sqrt(jnp.sum(taps * taps, axis=0)) / jnp.sum(taps, axis=0)
    noise = jnp.clip(jax.random.normal(jax.random.fold_in(key, 67), (FRAME_LENGTH, STATE), jnp.float32), -6.0, 6.0)
    flagged, _ = pulse_plan(key)
    nearby = flagged
    for lead in range(1, KCONV):
        nearby = nearby | jnp.concatenate([flagged[lead:], jnp.zeros((lead,), bool)])
    values = jnp.where(nearby[:, None], 0.003 * noise, noise + offset[None, :])
    return values.astype(jnp.bfloat16)


def draw_a_log(key, part):
    first, second, third = jax.random.split(jax.random.fold_in(key, 11), 3)
    step_mean = head_step_mean(key)
    share = 0.5
    slow = jax.random.uniform(first, (HEADS,), jnp.float32) < share
    keep = jax.random.uniform(second, (HEADS,), jnp.float32, 0.5, 2.0)
    slow_rate = keep / (step_mean * FRAME_LENGTH)
    reach = jax.random.uniform(third, (HEADS,), jnp.float32, 30.0, 50.0)
    fast_rate = 2.3 / (reach * step_mean)
    return jnp.log(jnp.where(slow, slow_rate, fast_rate)).astype(jnp.float32)


def draw_dt_raw(key, part):
    first, second = jax.random.split(jax.random.fold_in(key, 23), 2)
    cluster_total = FRAME_LENGTH // SEQ_SPAN_LOCAL
    noise = jnp.clip(0.4 * jax.random.normal(first, (FRAME_LENGTH, HEADS), jnp.float32), -0.75, 0.75)
    base = -4.75 + head_offsets(key)[None, :] + noise
    level = jax.random.uniform(second, (cluster_total,), jnp.float32, -0.8, 0.8)
    rows = jnp.arange(FRAME_LENGTH)
    cluster_table = rows // SEQ_SPAN_LOCAL
    flagged, depth_rows = pulse_plan(key)
    step_mean = head_step_mean(key)
    pulse_step = -jnp.log(1.0 - depth_rows)[:, None] * step_mean[None, :] * FRAME_LENGTH / 1.25
    pulse_raw = pulse_step + jnp.log(-jnp.expm1(-pulse_step))
    element_item = base + level[cluster_table][:, None]
    element_item = jnp.where(flagged[:, None], pulse_raw, element_item)
    return element_item.astype(jnp.float32)


def block_scale(stream_key, shape, cuts, smallest, largest):
    def one(dim, parts):
        heights = jax.random.uniform(jax.random.fold_in(jax.random.fold_in(stream_key, 6), dim), (parts,), jnp.float32, smallest / len(cuts), largest / len(cuts))
        return jnp.repeat(jnp.exp(heights), shape[dim] // parts).reshape((-1,) + (1,) * (len(shape) - dim - 1))

    gain = one(*cuts[0])
    for cut in cuts[1:]:
        gain = gain * one(*cut)
    return gain


def scatter_about(key, dims, deviation, most, cuts=(), held_as=jnp.bfloat16):
    factor_of = block_scale(key, dims, cuts, -0.22, 0.18) if cuts else 1.0
    values = jax.random.normal(key, dims, jnp.float32) * deviation * factor_of
    return jnp.minimum(jnp.maximum(values, -most), most).astype(held_as)


def setup_inputs(seed: int = 0) -> dict:
    key_list = jax.random.split(jax.random.key(seed), 12)
    x_in = scatter_about(key_list[0], (FRAME_LENGTH, INNER), 1.0, 6.0, ((0, 8), (1, 4)))
    z_gate = scatter_about(key_list[1], (FRAME_LENGTH, INNER), 1.0, 6.0, ((0, 8), (1, 4)))
    b_in = draw_b_in(jax.random.fold_in(key_list[11], 71), 0)
    c_in = scatter_about(key_list[3], (FRAME_LENGTH, STATE), 1.0, 6.0, ((0, 8),))
    dt_raw = draw_dt_raw(jax.random.fold_in(key_list[11], 71), 0)
    a_log = draw_a_log(jax.random.fold_in(key_list[11], 71), 0)
    d_skip = jnp.clip(0.5 + 1.0 * jax.random.uniform(key_list[6], (HEADS,), jnp.float32) ** block_scale(key_list[6], (HEADS,), ((0, 4),), -0.2, 0.2), 0.5, 1.5)
    conv_x = scatter_about(key_list[7], (KCONV, INNER), KCONV ** -0.5, 3.0, ((1, 4),), jnp.float32)
    conv_bc = draw_conv_bc(jax.random.fold_in(key_list[11], 71), 0)
    norm_gain = jnp.clip(1.0 + 0.18 * jax.random.normal(key_list[9], (INNER,), jnp.float32), 0.1, 1.9)
    w_out = scatter_about(key_list[10], (INNER, D), INNER ** -0.5, 0.0625, ((0, 4),))
    return {"x_in": x_in, "z_gate": z_gate, "b_in": b_in, "c_in": c_in, "dt_raw": dt_raw, "a_log": a_log, "d_skip": d_skip, "conv_x": conv_x, "conv_bc": conv_bc, "norm_gain": norm_gain, "w_out": w_out}


def causal_conv(values, rim, weight):
    n_rows = values.shape[0]
    padded = jnp.concatenate([rim.astype(jnp.float32), values.astype(jnp.float32)], axis=0)
    result = weight[0][None, :] * padded[0:n_rows]
    for offset in range(1, weight.shape[0]):
        result = result + weight[offset][None, :] * padded[offset:offset + n_rows]
    return jax.nn.silu(result).astype(jnp.bfloat16)

def span_step(memory, pieces):
    x_part, b_part, c_part, step_part, decay_part = pieces
    running = jnp.cumsum(decay_part, axis=0)
    length = x_part.shape[0]
    positions = lax.iota(jnp.int32, length)
    causal = positions[:, None] >= positions[None, :]
    spread = jnp.where(causal[:, :, None], running[:, None, :] - running[None, :, :], -1e+30)
    scores = jnp.dot(c_part, b_part.T, preferred_element_type=jnp.float32)
    b_wide = b_part.astype(jnp.float32)
    c_wide = c_part.astype(jnp.float32)
    mixing = jnp.exp(spread) * scores[:, :, None] * step_part[None, :, :]
    inside = jnp.einsum('ijh,jhp->ihp', mixing, x_part, precision=lax.Precision.HIGHEST)
    earlier = jnp.einsum('in,hpn->ihp', c_wide, memory, precision=lax.Precision.HIGHEST) * jnp.exp(running)[:, :, None]
    final_decay = running[length - 1]
    weights = jnp.exp(final_decay[None, :] - running) * step_part
    update = jnp.einsum('jhp,jn->hpn', x_part * weights[:, :, None], b_wide, precision=lax.Precision.HIGHEST)
    new_memory = memory * jnp.exp(final_decay)[:, None, None] + update
    return (new_memory, inside + earlier)

def reference(x_in, z_gate, b_in, c_in, dt_raw, a_log, d_skip, conv_x, conv_bc, norm_gain, w_out):
    rim_rows = conv_x.shape[0] - 1
    x_conv = causal_conv(x_in, jnp.zeros((rim_rows, x_in.shape[1]), jnp.bfloat16), conv_x)
    bc_in = jnp.concatenate([b_in, c_in], axis=1)
    bc_conv = causal_conv(bc_in, jnp.zeros((rim_rows, bc_in.shape[1]), jnp.bfloat16), conv_bc)
    b_conv = bc_conv[:, :STATE]
    c_conv = bc_conv[:, STATE:]
    dt_step = jax.nn.softplus(dt_raw)
    log_decay = -jnp.exp(a_log)[None, :] * dt_step
    x_heads = x_conv.astype(jnp.float32).reshape(FRAME_LENGTH, HEADS, HEAD_DIM)
    blocks = FRAME_LENGTH // SPAN

    def split_blocks(values):
        return values.reshape((blocks, SPAN) + values.shape[1:])
    start = jnp.zeros((HEADS, HEAD_DIM, STATE), jnp.float32)
    _, outputs = lax.scan(span_step, start, (split_blocks(x_heads), split_blocks(b_conv), split_blocks(c_conv), split_blocks(dt_step), split_blocks(log_decay)))
    ssd = outputs.reshape(FRAME_LENGTH, HEADS, HEAD_DIM) + d_skip[None, :, None] * x_heads
    gated = ssd.reshape(FRAME_LENGTH, INNER) * jax.nn.silu(z_gate.astype(jnp.float32))
    squares = lax.optimization_barrier(jnp.sum(gated * gated, axis=1))
    normed = (gated * lax.rsqrt(squares / INNER + 1e-05)[:, None] * norm_gain[None, :]).astype(jnp.bfloat16)
    group = INNER // N_HEAD

    def add_group(summed, index):
        piece = lax.dynamic_slice_in_dim(normed, index * group, group, 1)
        rows_w = lax.dynamic_slice_in_dim(w_out, index * group, group, 0)
        term = jnp.dot(piece, rows_w, preferred_element_type=jnp.float32).astype(jnp.bfloat16)
        term = lax.optimization_barrier(term)
        return (summed + term.astype(jnp.float32), None)
    summed, _ = lax.scan(add_group, jnp.zeros((FRAME_LENGTH, D), jnp.float32), jnp.arange(N_HEAD, dtype=jnp.int32))
    return summed.astype(jnp.bfloat16)
```

```python
import functools

import jax
import jax.numpy as jnp
from jax import lax
from jax.experimental import pallas as pl
from jax.experimental.pallas import tpu as pltpu
from jax.sharding import PartitionSpec as P

HEAD_DIM = 64
INNER = 8192
NORM_EPS = 1e-05
MESH = pl.DeviceIdType.MESH

CHUNK = 128
RIM = 16
TILE = 512
LANES = 128


def silu(v):
    return v / (1.0 + jnp.exp(-v))


def remote(src, dst, send, recv, **where):
    return pltpu.make_async_remote_copy(
        src_ref=src, dst_ref=dst, send_sem=send, recv_sem=recv, device_id=where, device_id_type=MESH
    )


def kernel(
    n_seq, n_head,
    x_hbm, z_hbm, b_hbm, c_hbm, w_hbm, dt_ref, rate_ref, skip_ref, cx_ref, cbc_ref, gain_ref,
    out_ref,
    x_v, z_v, w_v, bc_v, y_v, s_v, f_v, carry_in, carry_out, spread_v, pad_v, padbc_v,
    cs_v, dt_v, cst_v, dtt_v, tot_v, dev_v, sq_v, sq_in, send_v, mid_v, recv_v,
    load_sem, rim_send, rim_recv, carry_send, carry_recv, sq_send, sq_recv,
    out_send, mid_recv, fin_recv,
):
    rows, chans = z_v.shape
    heads = chans // HEAD_DIM
    chunks = rows // CHUNK
    own_rows = rows // n_head
    tiles = w_v.shape[1] // TILE
    pieces = carry_send.shape[0]
    piece = chans // pieces
    seq = lax.axis_index("seq")
    head = lax.axis_index("head")
    state = b_hbm.shape[1]

    loads = [
        pltpu.make_async_copy(x_hbm, x_v.at[pl.ds(RIM, rows)], load_sem.at[0]),
        pltpu.make_async_copy(b_hbm, bc_v.at[pl.ds(RIM, rows), pl.ds(0, state)], load_sem.at[1]),
        pltpu.make_async_copy(c_hbm, bc_v.at[pl.ds(RIM, rows), pl.ds(state, state)], load_sem.at[2]),
        pltpu.make_async_copy(z_hbm, z_v, load_sem.at[3]),
        pltpu.make_async_copy(w_hbm, w_v, load_sem.at[4]),
    ]
    for copy in loads:
        copy.start()

    barrier = pltpu.get_barrier_semaphore()
    for s in range(1, n_head):
        pl.semaphore_signal(barrier, inc=1, device_id={"head": lax.rem(head + s, n_head)}, device_id_type=MESH)

    for s in (1, n_seq - 1):
        pl.semaphore_signal(barrier, inc=1, device_id={"seq": lax.rem(seq + s, n_seq)}, device_id_type=MESH)
    pl.semaphore_wait(barrier, n_head + 1)

    tail = pl.ds(rows - RIM, RIM)
    rims = [
        remote(x_hbm.at[tail], x_v.at[pl.ds(0, RIM)], rim_send.at[0], rim_recv.at[0], seq=seq + 1),
        remote(b_hbm.at[tail], bc_v.at[pl.ds(0, RIM), pl.ds(0, state)], rim_send.at[1], rim_recv.at[1], seq=seq + 1),
        remote(c_hbm.at[tail], bc_v.at[pl.ds(0, RIM), pl.ds(state, state)], rim_send.at[2], rim_recv.at[2], seq=seq + 1),
    ]

    @pl.when(seq < n_seq - 1)
    def _():
        for copy in rims:
            copy.start()

    @pl.when(seq == 0)
    def _():
        x_v[0:RIM, :] = jnp.zeros((RIM, chans), jnp.bfloat16)
        bc_v[0:RIM, :] = jnp.zeros((RIM, 2 * state), jnp.bfloat16)
        carry_in[...] = jnp.zeros_like(carry_in)

    of_lane = lax.broadcasted_iota(jnp.int32, (2 * LANES, chans), 1) // HEAD_DIM
    of_row = lax.broadcasted_iota(jnp.int32, (2 * LANES, chans), 0) % LANES
    spread_v[...] = jnp.where(of_lane == of_row, 1.0, 0.0).astype(jnp.bfloat16)
    dt_v[...] = jnp.zeros_like(dt_v)
    dt_v[:, 0:heads] = dt_ref[...]
    f_v[...] = jnp.zeros_like(f_v)
    dev_v[...] = jnp.ones_like(dev_v)

    row_id = lax.broadcasted_iota(jnp.int32, (CHUNK, CHUNK), 0)
    col_id = lax.broadcasted_iota(jnp.int32, (CHUNK, CHUNK), 1)
    causal = row_id >= col_id

    def over_channels(values):
        high = values.astype(jnp.bfloat16)
        low = (values - high.astype(jnp.float32)).astype(jnp.bfloat16)
        return jnp.dot(
            jnp.concatenate([high, low], axis=1), spread_v[...], preferred_element_type=jnp.float32
        )

    def conv(values_ref, padded, start, taps):
        padded[0:8, :] = values_ref[pl.ds(start, RIM), :].astype(jnp.float32)[8:16]
        padded[8 : 8 + CHUNK, :] = values_ref[pl.ds(start + RIM, CHUNK), :].astype(jnp.float32)
        total = taps[0:1, :] * padded[5 : 5 + CHUNK, :]
        for k in range(1, 4):
            total = total + taps[k : k + 1, :] * padded[5 + k : 5 + k + CHUNK, :]
        values_ref[pl.ds(start + RIM, CHUNK), :] = silu(total).astype(jnp.bfloat16)

    for copy in loads[:3]:
        copy.wait()

    def state_step(i, _):
        c = chunks - 1 - i
        start = pl.multiple_of(c * CHUNK, CHUNK)

        @pl.when((c == 0) & (seq > 0))
        def _():
            for copy in rims:
                copy.wait_recv()

        conv(x_v, pad_v, start, cx_ref)
        conv(bc_v, padbc_v, start, cbc_ref)
        raw = dt_v[pl.ds(start, CHUNK), :]
        dt = jnp.maximum(raw, 0.0) + jnp.log1p(jnp.exp(-jnp.abs(raw)))
        decay = -jnp.exp(rate_ref[...]) * dt
        running = jnp.dot(
            jnp.where(causal, 1.0, 0.0), decay,
            precision=lax.Precision.HIGHEST, preferred_element_type=jnp.float32,
        )
        dt_v[pl.ds(start, CHUNK), :] = dt
        cs_v[pl.ds(start, CHUNK), :] = running
        cst_v[pl.ds(start, CHUNK), :] = running.T
        dtt_v[pl.ds(start, CHUNK), :] = dt.T
        last = running[CHUNK - 1 : CHUNK, :]
        end = over_channels(jnp.broadcast_to(jnp.exp(last), (8, LANES)))
        tot_v[pl.ds(pl.multiple_of(c * 8, 8), 8), :] = end
        weights = over_channels(jnp.exp(last - running) * dt)
        xw = (weights * x_v[pl.ds(start + RIM, CHUNK), :].astype(jnp.float32)).astype(jnp.bfloat16)
        b_t = bc_v[pl.ds(start + RIM, CHUNK), 0:state].astype(jnp.float32).T.astype(jnp.bfloat16)
        update = jnp.dot(b_t, xw, preferred_element_type=jnp.float32)
        s_v[pl.ds(pl.multiple_of(c * state, state), state), :] = update.astype(jnp.bfloat16)
        f_v[...] += dev_v[0:1, :] * update
        dev_v[...] = dev_v[...] * end
        return 0

    lax.fori_loop(0, chunks, state_step, 0)

    def carry_copy(k):
        columns = pl.ds(k * piece, piece)
        return remote(
            carry_out.at[:, columns], carry_in.at[:, columns], carry_send.at[k], carry_recv.at[k], seq=seq + 1
        )

    def within(c, _):
        @pl.when(c == seq * chunks // n_seq)
        def _():
            for k in range(pieces):
                @pl.when(seq > 0)
                def _():
                    carry_copy(k).wait_recv()

                @pl.when(seq < n_seq - 1)
                def _():
                    columns = slice(k * piece, (k + 1) * piece)
                    carry_out[:, columns] = (
                        dev_v[0:1, columns] * carry_in[:, columns].astype(jnp.float32) + f_v[:, columns]
                    ).astype(jnp.bfloat16)
                    carry_copy(k).start()

        start = pl.multiple_of(c * CHUNK, CHUNK)
        b = bc_v[pl.ds(start + RIM, CHUNK), 0:state]
        cc = bc_v[pl.ds(start + RIM, CHUNK), state : 2 * state]
        scores = lax.dot_general(cc, b, (((1,), (1,)), ((), ())), preferred_element_type=jnp.float32)
        scores = jnp.where(causal, scores, 0.0)
        running = cs_v[pl.ds(start, CHUNK), :]
        across = cst_v[pl.ds(start, CHUNK), :]
        steps = dtt_v[pl.ds(start, CHUNK), :]
        left = lax.broadcasted_iota(jnp.int32, (CHUNK, LANES), 1) < HEAD_DIM
        zero = jnp.zeros((CHUNK, LANES), jnp.bfloat16)
        for pair in range(heads // 2):
            mixes = []
            for h in (2 * pair, 2 * pair + 1):
                gap = running[:, h : h + 1] - across[h : h + 1, :]
                mix = jnp.exp(jnp.minimum(gap, 0.0)) * (scores * steps[h : h + 1, :])
                mixes.append(mix.astype(jnp.bfloat16))
            lanes = slice(pair * LANES, (pair + 1) * LANES)
            xp = x_v[pl.ds(start + RIM, CHUNK), lanes]
            both = jnp.concatenate([jnp.where(left, xp, zero), jnp.where(left, zero, xp)], axis=0)
            y_v[pl.ds(start, CHUNK), lanes] = jnp.dot(
                jnp.concatenate(mixes, axis=1), both, preferred_element_type=jnp.float32
            )
        return 0

    lax.fori_loop(0, chunks, within, 0)

    f_v[...] = carry_in[...].astype(jnp.float32)

    def starts(c, _):
        here = pl.ds(pl.multiple_of(c * state, state), state)
        update = s_v[here, :].astype(jnp.float32)
        now = f_v[...]
        s_v[here, :] = now.astype(jnp.bfloat16)
        f_v[...] = now * tot_v[pl.ds(pl.multiple_of(c * 8, 8), 8), :][0:1, :] + update
        return 0

    lax.fori_loop(0, chunks, starts, 0)
    loads[3].wait()

    def gate(c):
        start = pl.multiple_of(c * CHUNK, CHUNK)
        here = pl.ds(start, CHUNK)
        cc = bc_v[pl.ds(start + RIM, CHUNK), state : 2 * state]
        grown = over_channels(jnp.exp(cs_v[here, :]))
        earlier = jnp.dot(
            cc, s_v[pl.ds(pl.multiple_of(c * state, state), state), :], preferred_element_type=jnp.float32
        )
        x = x_v[pl.ds(start + RIM, CHUNK), :].astype(jnp.float32)
        ssd = y_v[here, :] + earlier * grown + skip_ref[...] * x
        gated = ssd * silu(z_v[here, :].astype(jnp.float32))
        z_v[here, :] = (gated * gain_ref[...]).astype(jnp.bfloat16)
        squares = gated * gated
        total = squares[:, 0:LANES]
        for g in range(1, chans // LANES):
            total = total + squares[:, g * LANES : (g + 1) * LANES]
        sq_v[here, :] = total

    def product(block, t):
        columns = pl.ds(pl.multiple_of(t * TILE, TILE), TILE)
        here = pl.ds(pl.multiple_of(block * own_rows, own_rows), own_rows)
        return jnp.dot(z_v[here, :], w_v[:, columns], preferred_element_type=jnp.float32)

    def sq_copy(s):
        target = lax.rem(head + s, n_head)
        here = pl.ds(pl.multiple_of(target * own_rows, own_rows), own_rows)
        return remote(sq_v.at[here], sq_in.at[s - 1], sq_send.at[s - 1], sq_recv.at[s - 1], head=target)

    def finish(slots):
        here = pl.ds(pl.multiple_of(head * own_rows, own_rows), own_rows)
        squares = sq_v[here, :]
        for s in range(1, n_head):
            sq_copy(s).wait_recv()
            squares = squares + sq_in[s - 1]
        scale = lax.rsqrt(jnp.sum(squares, axis=1, keepdims=True) / INNER + NORM_EPS)
        sq_v[here, :] = jnp.broadcast_to(scale, (own_rows, LANES))

        def last(t, _):
            total = product(head, t)
            for slot in range(slots):
                fin_copy(slot, t).wait_recv()
                total = total + recv_v[slot, t].astype(jnp.float32)
            columns = pl.ds(pl.multiple_of(t * TILE, TILE), TILE)
            scale = sq_v[here, :][:, 0:1]
            out_ref[:, columns] = (total * scale).astype(jnp.bfloat16)
            return 0

        lax.fori_loop(0, tiles, last, 0)

    if n_head == 4:
        by_x = head + 1 - 2 * lax.rem(head, 2)
        by_y = lax.rem(head + 2, 4)
        far = 3 - head
        half = tiles // 2
        per_block = own_rows // CHUNK

        def gates(block):
            lax.fori_loop(0, per_block, lambda i, _: (gate(block * per_block + i), 0)[1], 0)

        def mid_copy(t, target):
            return remote(send_v.at[0, t], mid_v.at[t], out_send.at[0, t], mid_recv.at[t], head=target)

        def fin_copy(slot, t):
            return remote(
                send_v.at[slot + 1, t], recv_v.at[slot, t], out_send.at[slot + 1, t], fin_recv.at[slot, t],
                head=by_x if slot == 0 else by_y,
            )

        gates(far)
        loads[4].wait()

        def first(i, _):
            send_v[0, i] = product(far, i).astype(jnp.bfloat16)
            mid_copy(i, by_x).start()
            send_v[0, i + half] = product(far, i + half).astype(jnp.bfloat16)
            mid_copy(i + half, by_y).start()
            return 0

        lax.fori_loop(0, half, first, 0)
        gates(by_x)
        gates(by_y)

        def plain(i, _):
            send_v[1, i] = product(by_x, i).astype(jnp.bfloat16)
            fin_copy(0, i).start()
            send_v[2, i + half] = product(by_y, i + half).astype(jnp.bfloat16)
            fin_copy(1, i + half).start()
            return 0

        lax.fori_loop(0, half, plain, 0)
        gates(head)
        for s in range(1, n_head):
            sq_copy(s).start()

        def relayed(i, _):
            mine = product(by_x, i + half)
            mid_copy(i + half, by_y).wait_recv()
            send_v[1, i + half] = (mine + mid_v[i + half].astype(jnp.float32)).astype(jnp.bfloat16)
            fin_copy(0, i + half).start()
            mine = product(by_y, i)
            mid_copy(i, by_x).wait_recv()
            send_v[2, i] = (mine + mid_v[i].astype(jnp.float32)).astype(jnp.bfloat16)
            fin_copy(1, i).start()
            return 0

        lax.fori_loop(0, half, relayed, 0)
        finish(2)

        def sent(t, _):
            fin_copy(0, t).wait_send()
            fin_copy(1, t).wait_send()
            mid_copy(t, by_x).wait_send()
            return 0

        lax.fori_loop(0, tiles, sent, 0)
    else:
        def fin_copy(slot, t):
            return remote(
                send_v.at[slot, t], recv_v.at[slot, t], out_send.at[slot, t], fin_recv.at[slot, t],
                head=lax.rem(head + slot + 1, n_head),
            )

        lax.fori_loop(0, chunks, lambda c, _: (gate(c), 0)[1], 0)
        loads[4].wait()
        for s in range(1, n_head):
            sq_copy(s).start()

        def each(slot, _):
            def tile(t, _):
                send_v[slot, t] = product(lax.rem(head + slot + 1, n_head), t).astype(jnp.bfloat16)
                fin_copy(slot, t).start()
                return 0

            return lax.fori_loop(0, tiles, tile, 0)

        lax.fori_loop(0, n_head - 1, each, 0)
        finish(n_head - 1)

        def sent(slot, _):
            def tile(t, _):
                fin_copy(slot, t).wait_send()
                return 0

            return lax.fori_loop(0, tiles, tile, 0)

        lax.fori_loop(0, n_head - 1, sent, 0)

    for s in range(1, n_head):
        sq_copy(s).wait_send()

    @pl.when(seq < n_seq - 1)
    def _():
        for copy in rims:
            copy.wait_send()
        for k in range(pieces):
            carry_copy(k).wait_send()


def local(n_seq, n_head, x_in, z_gate, b_in, c_in, dt_raw, a_log, d_skip, conv_x, conv_bc, norm_gain, w_out):
    rows, chans = x_in.shape
    state = b_in.shape[1]
    width = w_out.shape[1]
    own = rows // n_head
    tiles = width // TILE
    chunks = rows // CHUNK
    pieces = 4
    heads = a_log.shape[0]
    rate = jnp.pad(a_log, (0, LANES - heads))[None, :]
    skip = jnp.repeat(d_skip, HEAD_DIM)[None, :]
    sends, mids, slots = (3, tiles, 2) if n_head == 4 else (n_head - 1, 1, n_head - 1)
    bf, f32 = jnp.bfloat16, jnp.float32
    any_spec = pl.BlockSpec(memory_space=pl.ANY)
    vmem = pl.BlockSpec(memory_space=pltpu.VMEM)
    dma = pltpu.SemaphoreType.DMA
    flops = 2 * rows * chans * (width + 3 * state)
    return pl.pallas_call(
        functools.partial(kernel, n_seq, n_head),
        out_shape=jax.ShapeDtypeStruct((own, width), bf),
        in_specs=[any_spec] * 5 + [vmem] * 6,
        out_specs=vmem,
        scratch_shapes=[
            pltpu.VMEM((RIM + rows, chans), bf),
            pltpu.VMEM((rows, chans), bf),
            pltpu.VMEM((chans, width), bf),
            pltpu.VMEM((RIM + rows, 2 * state), bf),
            pltpu.VMEM((rows, chans), f32),
            pltpu.VMEM((chunks * state, chans), bf),
            pltpu.VMEM((state, chans), f32),
            pltpu.VMEM((state, chans), bf),
            pltpu.VMEM((state, chans), bf),
            pltpu.VMEM((2 * LANES, chans), bf),
            pltpu.VMEM((8 + CHUNK, chans), f32),
            pltpu.VMEM((8 + CHUNK, 2 * state), f32),
            pltpu.VMEM((rows, LANES), f32),
            pltpu.VMEM((rows, LANES), f32),
            pltpu.VMEM((chunks * LANES, CHUNK), f32),
            pltpu.VMEM((chunks * LANES, CHUNK), f32),
            pltpu.VMEM((chunks * 8, chans), f32),
            pltpu.VMEM((8, chans), f32),
            pltpu.VMEM((rows, LANES), f32),
            pltpu.VMEM((n_head - 1, own, LANES), f32),
            pltpu.VMEM((sends, tiles, own, TILE), bf),
            pltpu.VMEM((mids, own, TILE), bf),
            pltpu.VMEM((slots, tiles, own, TILE), bf),
            dma((5,)), dma((3,)), dma((3,)), dma((pieces,)), dma((pieces,)),
            dma((n_head - 1,)), dma((n_head - 1,)),
            dma((sends, tiles)), dma((mids,)), dma((slots, tiles)),
        ],
        compiler_params=pltpu.CompilerParams(
            collective_id=0, has_side_effects=True, vmem_limit_bytes=62 * 1024 * 1024
        ),
        cost_estimate=pl.CostEstimate(
            flops=flops, bytes_accessed=2 * (2 * rows * chans + chans * width), transcendentals=rows * chans
        ),
    )(x_in, z_gate, b_in, c_in, w_out, dt_raw, rate, skip, conv_x, conv_bc, norm_gain[None, :])


def solution(mesh):
    in_specs = (
        P("seq", "head"), P("seq", "head"), P("seq", None), P("seq", None), P("seq", "head"),
        P("head"), P("head"), P(None, "head"), P(), P("head"), P("head", None),
    )
    body = functools.partial(local, mesh.shape["seq"], mesh.shape["head"])
    return jax.shard_map(
        body, mesh=mesh, in_specs=in_specs, out_specs=P(("seq", "head"), None), check_vma=False
    )
```

```python
import functools

import jax
import jax.numpy as jnp
from jax import lax
from jax.experimental import pallas as pl
from jax.experimental.pallas import tpu as pltpu
from jax.sharding import PartitionSpec as P

HEAD_DIM = 64
INNER = 8192
NORM_EPS = 1e-05
MESH = pl.DeviceIdType.MESH

CHUNK = 128
RIM = 16
TILE = 512
LANES = 128


def silu(v):
    half = 0.5 * v
    return half + half * jnp.tanh(half)


def remote(src, dst, send, recv, **where):
    return pltpu.make_async_remote_copy(
        src_ref=src, dst_ref=dst, send_sem=send, recv_sem=recv, device_id=where, device_id_type=MESH
    )


def kernel(
    n_seq, n_head,
    x_hbm, z_hbm, b_hbm, c_hbm, w_hbm, dt_ref, rate_ref, skip_ref, cx_ref, cbc_ref, gain_ref,
    out_ref,
    x_v, z_v, w_v, bc_v, y_v, s_v, f_v, carry_in, carry_out, spread_v, pad_v, padbc_v,
    cs_v, rate_v, skip_v, cst_v, dtt_v, tot_v, dev_v, sq_v, sq_in, send_v, mid_v, recv_v,
    load_sem, rim_send, rim_recv, carry_send, carry_recv, sq_send, sq_recv,
    out_send, mid_recv, fin_recv,
):
    rows, chans = z_v.shape
    heads = chans // HEAD_DIM
    chunks = rows // CHUNK
    own_rows = rows // n_head
    tiles = w_v.shape[1] // TILE
    pieces = carry_send.shape[0]
    piece = chans // pieces
    seq = lax.axis_index("seq")
    head = lax.axis_index("head")
    state = b_hbm.shape[1]

    loads = [
        pltpu.make_async_copy(x_hbm, x_v.at[pl.ds(RIM, rows)], load_sem.at[0]),
        pltpu.make_async_copy(b_hbm, bc_v.at[pl.ds(RIM, rows), pl.ds(0, state)], load_sem.at[1]),
        pltpu.make_async_copy(c_hbm, bc_v.at[pl.ds(RIM, rows), pl.ds(state, state)], load_sem.at[2]),
        pltpu.make_async_copy(z_hbm, z_v, load_sem.at[3]),
        pltpu.make_async_copy(w_hbm, w_v, load_sem.at[4]),
    ]
    for copy in loads:
        copy.start()

    barrier = pltpu.get_barrier_semaphore()
    for s in range(1, n_head):
        pl.semaphore_signal(barrier, inc=1, device_id={"head": lax.rem(head + s, n_head)}, device_id_type=MESH)

    for s in (1, n_seq - 1):
        pl.semaphore_signal(barrier, inc=1, device_id={"seq": lax.rem(seq + s, n_seq)}, device_id_type=MESH)
    pl.semaphore_wait(barrier, n_head + 1)

    tail = pl.ds(rows - RIM, RIM)
    rims = [
        remote(x_hbm.at[tail], x_v.at[pl.ds(0, RIM)], rim_send.at[0], rim_recv.at[0], seq=seq + 1),
        remote(b_hbm.at[tail], bc_v.at[pl.ds(0, RIM), pl.ds(0, state)], rim_send.at[1], rim_recv.at[1], seq=seq + 1),
        remote(c_hbm.at[tail], bc_v.at[pl.ds(0, RIM), pl.ds(state, state)], rim_send.at[2], rim_recv.at[2], seq=seq + 1),
    ]

    @pl.when(seq < n_seq - 1)
    def _():
        for copy in rims:
            copy.start()

    @pl.when(seq == 0)
    def _():
        x_v[0:RIM, :] = jnp.zeros((RIM, chans), jnp.bfloat16)
        bc_v[0:RIM, :] = jnp.zeros((RIM, 2 * state), jnp.bfloat16)
        carry_in[...] = jnp.zeros_like(carry_in)

    of_lane = lax.broadcasted_iota(jnp.int32, (2 * LANES, chans), 1) // HEAD_DIM
    of_row = lax.broadcasted_iota(jnp.int32, (2 * LANES, chans), 0) % LANES
    spread_v[...] = jnp.where(of_lane == of_row, 1.0, 0.0).astype(jnp.bfloat16)
    f_v[...] = jnp.zeros_like(f_v)
    dev_v[...] = jnp.ones_like(dev_v)

    row_id = lax.broadcasted_iota(jnp.int32, (CHUNK, CHUNK), 0)
    col_id = lax.broadcasted_iota(jnp.int32, (CHUNK, CHUNK), 1)
    causal = row_id >= col_id

    def over_channels(values):
        high = values.astype(jnp.bfloat16)
        low = (values - high.astype(jnp.float32)).astype(jnp.bfloat16)
        return jnp.dot(
            jnp.concatenate([high, low], axis=1), spread_v[...], preferred_element_type=jnp.float32
        )

    def conv(values_ref, padded, start, taps):
        padded[0:8, :] = values_ref[pl.ds(start, RIM), :].astype(jnp.float32)[8:16]
        padded[8 : 8 + CHUNK, :] = values_ref[pl.ds(start + RIM, CHUNK), :].astype(jnp.float32)
        total = taps[0:1, :] * padded[5 : 5 + CHUNK, :]
        for k in range(1, 4):
            total = total + taps[k : k + 1, :] * padded[5 + k : 5 + k + CHUNK, :]
        values_ref[pl.ds(start + RIM, CHUNK), :] = silu(total).astype(jnp.bfloat16)

    rate_v[...] = jnp.zeros_like(rate_v)
    rate_v[0:1, 0:heads] = skip_ref[...]
    skip_v[...] = over_channels(rate_v[0:8, :])
    rate_v[0:1, 0:heads] = jnp.exp(rate_ref[...])
    rate_v[...] = rate_v[...].T

    for copy in loads[:3]:
        copy.wait()

    def state_step(i, _):
        c = chunks - 1 - i
        start = pl.multiple_of(c * CHUNK, CHUNK)

        @pl.when((c == 0) & (seq > 0))
        def _():
            for copy in rims:
                copy.wait_recv()

        conv(x_v, pad_v, start, cx_ref)
        conv(bc_v, padbc_v, start, cbc_ref)
        raw = dt_ref[:, pl.ds(start, CHUNK)]
        steps = jnp.maximum(raw, 0.0) + jnp.log1p(jnp.exp(-jnp.abs(raw)))
        across = jnp.dot(
            -rate_v[0:heads, 0:1] * steps, jnp.where(row_id <= col_id, 1.0, 0.0),
            precision=lax.Precision.HIGHEST, preferred_element_type=jnp.float32,
        )
        of_heads = pl.ds(pl.multiple_of(c * heads, heads), heads)
        cst_v[of_heads, :] = across
        dtt_v[of_heads, :] = steps
        rest = jnp.zeros((LANES - heads, CHUNK), jnp.float32)
        running = jnp.concatenate([across, rest], axis=0).T
        dt = jnp.concatenate([steps, rest], axis=0).T
        cs_v[pl.ds(start, CHUNK), :] = running
        last = running[CHUNK - 1 : CHUNK, :]
        end = over_channels(jnp.broadcast_to(jnp.exp(last), (8, LANES)))
        tot_v[pl.ds(pl.multiple_of(c * 8, 8), 8), :] = end
        weights = over_channels(jnp.exp(last - running) * dt)
        xw = (weights * x_v[pl.ds(start + RIM, CHUNK), :].astype(jnp.float32)).astype(jnp.bfloat16)
        b_t = bc_v[pl.ds(start + RIM, CHUNK), 0:state].astype(jnp.float32).T.astype(jnp.bfloat16)
        update = jnp.dot(b_t, xw, preferred_element_type=jnp.float32)
        s_v[pl.ds(pl.multiple_of(c * state, state), state), :] = update.astype(jnp.bfloat16)
        f_v[...] += dev_v[0:1, :] * update
        dev_v[...] = dev_v[...] * end
        return 0

    lax.fori_loop(0, chunks, state_step, 0)

    def carry_copy(k):
        columns = pl.ds(k * piece, piece)
        return remote(
            carry_out.at[:, columns], carry_in.at[:, columns], carry_send.at[k], carry_recv.at[k], seq=seq + 1
        )

    def serve():
        for k in range(pieces):
            @pl.when(seq > 0)
            def _():
                carry_copy(k).wait_recv()

            @pl.when(seq < n_seq - 1)
            def _():
                columns = slice(k * piece, (k + 1) * piece)
                carry_out[:, columns] = (
                    dev_v[0:1, columns] * carry_in[:, columns].astype(jnp.float32) + f_v[:, columns]
                ).astype(jnp.bfloat16)
                carry_copy(k).start()

        f_v[...] = carry_in[...].astype(jnp.float32)

        def starts(c, _):
            here = pl.ds(pl.multiple_of(c * state, state), state)
            update = s_v[here, :].astype(jnp.float32)
            now = f_v[...]
            s_v[here, :] = now.astype(jnp.bfloat16)
            f_v[...] = now * tot_v[pl.ds(pl.multiple_of(c * 8, 8), 8), :][0:1, :] + update
            return 0

        lax.fori_loop(0, chunks, starts, 0)
        loads[3].wait()

    def within(c):
        start = pl.multiple_of(c * CHUNK, CHUNK)
        b = bc_v[pl.ds(start + RIM, CHUNK), 0:state]
        cc = bc_v[pl.ds(start + RIM, CHUNK), state : 2 * state]
        scores = lax.dot_general(cc, b, (((1,), (1,)), ((), ())), preferred_element_type=jnp.float32)
        scores = jnp.where(causal, scores, 0.0)
        running = cs_v[pl.ds(start, CHUNK), :]
        of_heads = pl.ds(pl.multiple_of(c * heads, heads), heads)
        across = cst_v[of_heads, :]
        steps = dtt_v[of_heads, :]
        left = lax.broadcasted_iota(jnp.int32, (CHUNK, LANES), 1) < HEAD_DIM
        zero = jnp.zeros((CHUNK, LANES), jnp.bfloat16)
        for pair in range(heads // 2):
            mixes = []
            for h in (2 * pair, 2 * pair + 1):
                gap = running[:, h : h + 1] - across[h : h + 1, :]
                mix = jnp.exp(jnp.minimum(gap, 0.0)) * (scores * steps[h : h + 1, :])
                mixes.append(mix.astype(jnp.bfloat16))
            lanes = slice(pair * LANES, (pair + 1) * LANES)
            xp = x_v[pl.ds(start + RIM, CHUNK), lanes]
            both = jnp.concatenate([jnp.where(left, xp, zero), jnp.where(left, zero, xp)], axis=0)
            y_v[pl.ds(start, CHUNK), lanes] = jnp.dot(
                jnp.concatenate(mixes, axis=1), both, preferred_element_type=jnp.float32
            )

    def gate(c):
        start = pl.multiple_of(c * CHUNK, CHUNK)
        here = pl.ds(start, CHUNK)
        cc = bc_v[pl.ds(start + RIM, CHUNK), state : 2 * state]
        grown = over_channels(jnp.exp(cs_v[here, :]))
        earlier = jnp.dot(
            cc, s_v[pl.ds(pl.multiple_of(c * state, state), state), :], preferred_element_type=jnp.float32
        )
        x = x_v[pl.ds(start + RIM, CHUNK), :].astype(jnp.float32)
        ssd = y_v[here, :] + earlier * grown + skip_v[0:1, :] * x
        gated = ssd * silu(z_v[here, :].astype(jnp.float32))
        z_v[here, :] = (gated * gain_ref[...]).astype(jnp.bfloat16)
        squares = gated * gated
        total = squares[:, 0:LANES]
        for g in range(1, chans // LANES):
            total = total + squares[:, g * LANES : (g + 1) * LANES]
        sq_v[here, :] = total

    def product(block, t):
        columns = pl.ds(pl.multiple_of(t * TILE, TILE), TILE)
        here = pl.ds(pl.multiple_of(block * own_rows, own_rows), own_rows)
        return jnp.dot(z_v[here, :], w_v[:, columns], preferred_element_type=jnp.float32)

    def sq_copy(s):
        target = lax.rem(head + s, n_head)
        here = pl.ds(pl.multiple_of(target * own_rows, own_rows), own_rows)
        return remote(sq_v.at[here], sq_in.at[s - 1], sq_send.at[s - 1], sq_recv.at[s - 1], head=target)

    def finish(slots):
        here = pl.ds(pl.multiple_of(head * own_rows, own_rows), own_rows)
        squares = sq_v[here, :]
        for s in range(1, n_head):
            sq_copy(s).wait_recv()
            squares = squares + sq_in[s - 1]
        scale = lax.rsqrt(jnp.sum(squares, axis=1, keepdims=True) / INNER + NORM_EPS)
        sq_v[here, :] = jnp.broadcast_to(scale, (own_rows, LANES))

        def last(t, _):
            total = product(head, t)
            for slot in range(slots):
                fin_copy(slot, t).wait_recv()
                total = total + recv_v[slot, t].astype(jnp.float32)
            columns = pl.ds(pl.multiple_of(t * TILE, TILE), TILE)
            scale = sq_v[here, :][:, 0:1]
            out_ref[:, columns] = (total * scale).astype(jnp.bfloat16)
            return 0

        lax.fori_loop(0, tiles, last, 0)

    if n_head == 4:
        by_x = head + 1 - 2 * lax.rem(head, 2)
        by_y = lax.rem(head + 2, 4)
        far = 3 - head
        half = tiles // 2
        per_block = own_rows // CHUNK

        def gates(block):
            lax.fori_loop(0, per_block, lambda i, _: (gate(block * per_block + i), 0)[1], 0)

        def mid_copy(t, target):
            return remote(send_v.at[0, t], mid_v.at[t], out_send.at[0, t], mid_recv.at[t], head=target)

        def fin_copy(slot, t):
            return remote(
                send_v.at[slot + 1, t], recv_v.at[slot, t], out_send.at[slot + 1, t], fin_recv.at[slot, t],
                head=by_x if slot == 0 else by_y,
            )

        def first(i, _):
            send_v[0, i] = product(far, i).astype(jnp.bfloat16)
            mid_copy(i, by_x).start()
            send_v[0, i + half] = product(far, i + half).astype(jnp.bfloat16)
            mid_copy(i + half, by_y).start()
            return 0

        turn = per_block + seq * (chunks - per_block) // n_seq

        def in_order(i, _):
            @pl.when(i == turn)
            def _():
                serve()
                gates(far)
                loads[4].wait()
                lax.fori_loop(0, half, first, 0)

            j = i // per_block
            block = 2 * lax.rem(head // 2 + j + 1, 2) + lax.rem(lax.rem(head, 2) + 1 + j // 2, 2)
            within(block * per_block + lax.rem(i, per_block))
            return 0

        lax.fori_loop(0, chunks, in_order, 0)
        gates(by_x)
        gates(by_y)

        def plain(i, _):
            send_v[1, i] = product(by_x, i).astype(jnp.bfloat16)
            fin_copy(0, i).start()
            send_v[2, i + half] = product(by_y, i + half).astype(jnp.bfloat16)
            fin_copy(1, i + half).start()
            return 0

        lax.fori_loop(0, half, plain, 0)
        gates(head)
        for s in range(1, n_head):
            sq_copy(s).start()

        def relayed(i, _):
            mine = product(by_x, i + half)
            mid_copy(i + half, by_y).wait_recv()
            send_v[1, i + half] = (mine + mid_v[i + half].astype(jnp.float32)).astype(jnp.bfloat16)
            fin_copy(0, i + half).start()
            mine = product(by_y, i)
            mid_copy(i, by_x).wait_recv()
            send_v[2, i] = (mine + mid_v[i].astype(jnp.float32)).astype(jnp.bfloat16)
            fin_copy(1, i).start()
            return 0

        lax.fori_loop(0, half, relayed, 0)
        finish(2)

        def sent(t, _):
            fin_copy(0, t).wait_send()
            fin_copy(1, t).wait_send()
            mid_copy(t, by_x).wait_send()
            return 0

        lax.fori_loop(0, tiles, sent, 0)
    else:
        def fin_copy(slot, t):
            return remote(
                send_v.at[slot, t], recv_v.at[slot, t], out_send.at[slot, t], fin_recv.at[slot, t],
                head=lax.rem(head + slot + 1, n_head),
            )

        def in_order(c, _):
            @pl.when(c == seq * chunks // n_seq)
            def _():
                serve()

            within(c)
            return 0

        lax.fori_loop(0, chunks, in_order, 0)
        lax.fori_loop(0, chunks, lambda c, _: (gate(c), 0)[1], 0)
        loads[4].wait()
        for s in range(1, n_head):
            sq_copy(s).start()

        def each(slot, _):
            def tile(t, _):
                send_v[slot, t] = product(lax.rem(head + slot + 1, n_head), t).astype(jnp.bfloat16)
                fin_copy(slot, t).start()
                return 0

            return lax.fori_loop(0, tiles, tile, 0)

        lax.fori_loop(0, n_head - 1, each, 0)
        finish(n_head - 1)

        def sent(slot, _):
            def tile(t, _):
                fin_copy(slot, t).wait_send()
                return 0

            return lax.fori_loop(0, tiles, tile, 0)

        lax.fori_loop(0, n_head - 1, sent, 0)

    for s in range(1, n_head):
        sq_copy(s).wait_send()

    @pl.when(seq < n_seq - 1)
    def _():
        for copy in rims:
            copy.wait_send()
        for k in range(pieces):
            carry_copy(k).wait_send()


def local(n_seq, n_head, x_in, z_gate, b_in, c_in, dt_raw, a_log, d_skip, conv_x, conv_bc, norm_gain, w_out):
    rows, chans = x_in.shape
    state = b_in.shape[1]
    width = w_out.shape[1]
    own = rows // n_head
    tiles = width // TILE
    chunks = rows // CHUNK
    pieces = min(8, chans // LANES)
    heads = a_log.shape[0]
    sends, mids, slots = (3, tiles, 2) if n_head == 4 else (n_head - 1, 1, n_head - 1)
    bf, f32 = jnp.bfloat16, jnp.float32
    any_spec = pl.BlockSpec(memory_space=pl.ANY)
    vmem = pl.BlockSpec(memory_space=pltpu.VMEM)
    dma = pltpu.SemaphoreType.DMA
    flops = 2 * rows * chans * (width + 3 * state)
    return pl.pallas_call(
        functools.partial(kernel, n_seq, n_head),
        out_shape=jax.ShapeDtypeStruct((own, width), bf),
        in_specs=[any_spec] * 5 + [vmem] * 6,
        out_specs=vmem,
        scratch_shapes=[
            pltpu.VMEM((RIM + rows, chans), bf),
            pltpu.VMEM((rows, chans), bf),
            pltpu.VMEM((chans, width), bf),
            pltpu.VMEM((RIM + rows, 2 * state), bf),
            pltpu.VMEM((rows, chans), f32),
            pltpu.VMEM((chunks * state, chans), bf),
            pltpu.VMEM((state, chans), f32),
            pltpu.VMEM((state, chans), bf),
            pltpu.VMEM((state, chans), bf),
            pltpu.VMEM((2 * LANES, chans), bf),
            pltpu.VMEM((8 + CHUNK, chans), f32),
            pltpu.VMEM((8 + CHUNK, 2 * state), f32),
            pltpu.VMEM((rows, LANES), f32),
            pltpu.VMEM((LANES, LANES), f32),
            pltpu.VMEM((8, chans), f32),
            pltpu.VMEM((chunks * heads, CHUNK), f32),
            pltpu.VMEM((chunks * heads, CHUNK), f32),
            pltpu.VMEM((chunks * 8, chans), f32),
            pltpu.VMEM((8, chans), f32),
            pltpu.VMEM((rows, LANES), f32),
            pltpu.VMEM((n_head - 1, own, LANES), f32),
            pltpu.VMEM((sends, tiles, own, TILE), bf),
            pltpu.VMEM((mids, own, TILE), bf),
            pltpu.VMEM((slots, tiles, own, TILE), bf),
            dma((5,)), dma((3,)), dma((3,)), dma((pieces,)), dma((pieces,)),
            dma((n_head - 1,)), dma((n_head - 1,)),
            dma((sends, tiles)), dma((mids,)), dma((slots, tiles)),
        ],
        compiler_params=pltpu.CompilerParams(
            collective_id=0, has_side_effects=True, vmem_limit_bytes=62 * 1024 * 1024
        ),
        cost_estimate=pl.CostEstimate(
            flops=flops, bytes_accessed=2 * (2 * rows * chans + chans * width), transcendentals=rows * chans
        ),
    )(x_in, z_gate, b_in, c_in, w_out, dt_raw.T, a_log[None, :], d_skip[None, :], conv_x, conv_bc, norm_gain[None, :])


def solution(mesh):
    in_specs = (
        P("seq", "head"), P("seq", "head"), P("seq", None), P("seq", None), P("seq", "head"),
        P("head"), P("head"), P(None, "head"), P(), P("head"), P("head", None),
    )
    body = functools.partial(local, mesh.shape["seq"], mesh.shape["head"])
    return jax.shard_map(
        body, mesh=mesh, in_specs=in_specs, out_specs=P(("seq", "head"), None), check_vma=False
    )
```

```python
import functools

import jax
import jax.numpy as jnp
from jax import lax
from jax.experimental import pallas as pl
from jax.experimental.pallas import tpu as pltpu
from jax.sharding import PartitionSpec as P

HEAD_DIM = 64
INNER = 8192
NORM_EPS = 1e-05
MESH = pl.DeviceIdType.MESH

CHUNK = 128
RIM = 16
TILE = 512
LANES = 128


def silu(v):
    half = 0.5 * v
    return half + half * jnp.tanh(half)


def remote(src, dst, send, recv, **where):
    return pltpu.make_async_remote_copy(
        src_ref=src, dst_ref=dst, send_sem=send, recv_sem=recv, device_id=where, device_id_type=MESH
    )


def kernel(
    n_seq, n_head,
    x_hbm, z_hbm, b_hbm, c_hbm, w_hbm, dt_ref, rate_ref, skip_ref, cx_ref, cbc_ref, gain_ref,
    out_ref,
    x_v, z_v, w_v, bc_v, y_v, s_v, f_v, carry_in, carry_out, pad_v, padbc_v,
    cs_v, rate_v, skip_v, cst_v, dtt_v, tot_v, dev_v, sq_v, sq_in, send_v, mid_v, recv_v,
    load_sem, rim_send, rim_recv, carry_send, carry_recv, sq_send, sq_recv,
    out_send, mid_recv, fin_recv,
):
    rows, chans = z_v.shape
    heads = chans // HEAD_DIM
    chunks = rows // CHUNK
    own_rows = rows // n_head
    tiles = w_v.shape[1] // TILE
    pieces = carry_send.shape[0]
    piece = chans // pieces
    seq = lax.axis_index("seq")
    head = lax.axis_index("head")
    state = b_hbm.shape[1]

    loads = [
        pltpu.make_async_copy(x_hbm, x_v.at[pl.ds(RIM, rows)], load_sem.at[0]),
        pltpu.make_async_copy(b_hbm, bc_v.at[pl.ds(RIM, rows), pl.ds(0, state)], load_sem.at[1]),
        pltpu.make_async_copy(c_hbm, bc_v.at[pl.ds(RIM, rows), pl.ds(state, state)], load_sem.at[2]),
        pltpu.make_async_copy(z_hbm, z_v, load_sem.at[3]),
        pltpu.make_async_copy(w_hbm, w_v, load_sem.at[4]),
    ]
    for copy in loads:
        copy.start()

    barrier = pltpu.get_barrier_semaphore()
    for s in range(1, n_head):
        pl.semaphore_signal(barrier, inc=1, device_id={"head": lax.rem(head + s, n_head)}, device_id_type=MESH)

    for s in (1, n_seq - 1):
        pl.semaphore_signal(barrier, inc=1, device_id={"seq": lax.rem(seq + s, n_seq)}, device_id_type=MESH)
    pl.semaphore_wait(barrier, n_head + 1)

    tail = pl.ds(rows - RIM, RIM)
    rims = [
        remote(x_hbm.at[tail], x_v.at[pl.ds(0, RIM)], rim_send.at[0], rim_recv.at[0], seq=seq + 1),
        remote(b_hbm.at[tail], bc_v.at[pl.ds(0, RIM), pl.ds(0, state)], rim_send.at[1], rim_recv.at[1], seq=seq + 1),
        remote(c_hbm.at[tail], bc_v.at[pl.ds(0, RIM), pl.ds(state, state)], rim_send.at[2], rim_recv.at[2], seq=seq + 1),
    ]

    @pl.when(seq < n_seq - 1)
    def _():
        for copy in rims:
            copy.start()

    @pl.when(seq == 0)
    def _():
        x_v[0:RIM, :] = jnp.zeros((RIM, chans), jnp.bfloat16)
        bc_v[0:RIM, :] = jnp.zeros((RIM, 2 * state), jnp.bfloat16)
        carry_in[...] = jnp.zeros_like(carry_in)

    f_v[...] = jnp.zeros_like(f_v)
    dev_v[...] = jnp.ones_like(dev_v)

    row_id = lax.broadcasted_iota(jnp.int32, (CHUNK, CHUNK), 0)
    col_id = lax.broadcasted_iota(jnp.int32, (CHUNK, CHUNK), 1)
    causal = row_id >= col_id

    left = lax.broadcasted_iota(jnp.int32, (CHUNK, LANES), 1) < HEAD_DIM
    groups = [slice(g, g + LANES) for g in range(0, chans, LANES)]

    def over_channels(values, g):
        return jnp.where(
            left[0 : values.shape[0]], values[:, 2 * g : 2 * g + 1], values[:, 2 * g + 1 : 2 * g + 2]
        )

    def conv(values_ref, padded, start, taps, lanes):
        padded[0:8, lanes] = values_ref[pl.ds(start, RIM), lanes].astype(jnp.float32)[8:16]
        padded[8 : 8 + CHUNK, lanes] = values_ref[pl.ds(start + RIM, CHUNK), lanes].astype(jnp.float32)
        total = taps[0:1, lanes] * padded[5 : 5 + CHUNK, lanes]
        for k in range(1, 4):
            total = total + taps[k : k + 1, lanes] * padded[5 + k : 5 + k + CHUNK, lanes]
        result = silu(total).astype(jnp.bfloat16)
        values_ref[pl.ds(start + RIM, CHUNK), lanes] = result
        return result

    rate_v[...] = jnp.zeros_like(rate_v)
    rate_v[0:1, 0:heads] = skip_ref[...]
    for g, lanes in enumerate(groups):
        skip_v[:, lanes] = over_channels(rate_v[0:8, :], g)
    rate_v[0:1, 0:heads] = jnp.exp(rate_ref[...])
    rate_v[...] = rate_v[...].T

    for copy in loads[:3]:
        copy.wait()

    def state_step(i, _):
        c = chunks - 1 - i
        start = pl.multiple_of(c * CHUNK, CHUNK)

        @pl.when((c == 0) & (seq > 0))
        def _():
            for copy in rims:
                copy.wait_recv()

        for g in range(0, 2 * state, LANES):
            conv(bc_v, padbc_v, start, cbc_ref, slice(g, g + LANES))
        raw = dt_ref[:, pl.ds(start, CHUNK)]
        steps = jnp.maximum(raw, 0.0) + jnp.log1p(jnp.exp(-jnp.abs(raw)))
        across = jnp.dot(
            -rate_v[0:heads, 0:1] * steps, jnp.where(row_id <= col_id, 1.0, 0.0),
            precision=lax.Precision.HIGHEST, preferred_element_type=jnp.float32,
        )
        of_heads = pl.ds(pl.multiple_of(c * heads, heads), heads)
        cst_v[of_heads, :] = across
        dtt_v[of_heads, :] = steps
        rest = jnp.zeros((LANES - heads, CHUNK), jnp.float32)
        running = jnp.concatenate([across, rest], axis=0).T
        dt = jnp.concatenate([steps, rest], axis=0).T
        cs_v[pl.ds(start, CHUNK), :] = running
        last = running[CHUNK - 1 : CHUNK, :]
        end = jnp.broadcast_to(jnp.exp(last), (8, LANES))
        weights = jnp.exp(last - running) * dt
        b_t = bc_v[pl.ds(start + RIM, CHUNK), 0:state].astype(jnp.float32).T.astype(jnp.bfloat16)
        ends = pl.ds(pl.multiple_of(c * 8, 8), 8)
        here = pl.ds(pl.multiple_of(c * state, state), state)
        for g in range(0, len(groups), 2):
            weighted = []
            for one in (g, g + 1):
                x = conv(x_v, pad_v, start, cx_ref, groups[one])
                tot_v[ends, groups[one]] = over_channels(end, one)
                weighted.append((over_channels(weights, one) * x.astype(jnp.float32)).astype(jnp.bfloat16))
            update = jnp.dot(b_t, jnp.concatenate(weighted, axis=1), preferred_element_type=jnp.float32)
            both = slice(g * LANES, (g + 2) * LANES)
            s_v[here, both] = update.astype(jnp.bfloat16)
            f_v[:, both] += dev_v[0:1, both] * update
            dev_v[:, both] = dev_v[:, both] * tot_v[ends, both]
        return 0

    lax.fori_loop(0, chunks, state_step, 0)

    def carry_copy(k):
        columns = pl.ds(k * piece, piece)
        return remote(
            carry_out.at[:, columns], carry_in.at[:, columns], carry_send.at[k], carry_recv.at[k], seq=seq + 1
        )

    def serve():
        for k in range(pieces):
            @pl.when(seq > 0)
            def _():
                carry_copy(k).wait_recv()

            @pl.when(seq < n_seq - 1)
            def _():
                columns = slice(k * piece, (k + 1) * piece)
                carry_out[:, columns] = (
                    dev_v[0:1, columns] * carry_in[:, columns].astype(jnp.float32) + f_v[:, columns]
                ).astype(jnp.bfloat16)
                carry_copy(k).start()

        f_v[...] = carry_in[...].astype(jnp.float32)

        def starts(c, _):
            here = pl.ds(pl.multiple_of(c * state, state), state)
            ends = pl.ds(pl.multiple_of(c * 8, 8), 8)
            for lanes in groups:
                update = s_v[here, lanes].astype(jnp.float32)
                now = f_v[:, lanes]
                s_v[here, lanes] = now.astype(jnp.bfloat16)
                f_v[:, lanes] = now * tot_v[ends, lanes][0:1, :] + update
            return 0

        lax.fori_loop(0, chunks, starts, 0)
        loads[3].wait()

    def within(c):
        start = pl.multiple_of(c * CHUNK, CHUNK)
        b = bc_v[pl.ds(start + RIM, CHUNK), 0:state]
        cc = bc_v[pl.ds(start + RIM, CHUNK), state : 2 * state]
        scores = lax.dot_general(cc, b, (((1,), (1,)), ((), ())), preferred_element_type=jnp.float32)
        scores = jnp.where(causal, scores, 0.0)
        running = cs_v[pl.ds(start, CHUNK), :]
        of_heads = pl.ds(pl.multiple_of(c * heads, heads), heads)
        across = cst_v[of_heads, :]
        steps = dtt_v[of_heads, :]
        zero = jnp.zeros((CHUNK, LANES), jnp.bfloat16)
        for pair in range(heads // 2):
            mixes = []
            for h in (2 * pair, 2 * pair + 1):
                gap = running[:, h : h + 1] - across[h : h + 1, :]
                mix = jnp.exp(jnp.minimum(gap, 0.0)) * (scores * steps[h : h + 1, :])
                mixes.append(mix.astype(jnp.bfloat16))
            lanes = slice(pair * LANES, (pair + 1) * LANES)
            xp = x_v[pl.ds(start + RIM, CHUNK), lanes]
            both = jnp.concatenate([jnp.where(left, xp, zero), jnp.where(left, zero, xp)], axis=0)
            y_v[pl.ds(start, CHUNK), lanes] = jnp.dot(
                jnp.concatenate(mixes, axis=1), both, preferred_element_type=jnp.float32
            )

    def gate(c):
        start = pl.multiple_of(c * CHUNK, CHUNK)
        here = pl.ds(start, CHUNK)
        cc = bc_v[pl.ds(start + RIM, CHUNK), state : 2 * state]
        grown = jnp.exp(cs_v[here, :])
        states = pl.ds(pl.multiple_of(c * state, state), state)
        total = jnp.zeros((CHUNK, LANES), jnp.float32)
        for g in range(0, len(groups), 2):
            both = slice(g * LANES, (g + 2) * LANES)
            earlier = jnp.dot(cc, s_v[states, both], preferred_element_type=jnp.float32)
            for one in (g, g + 1):
                lanes = groups[one]
                part = earlier[:, (one - g) * LANES : (one - g + 1) * LANES] * over_channels(grown, one)
                x = x_v[pl.ds(start + RIM, CHUNK), lanes].astype(jnp.float32)
                ssd = y_v[here, lanes] + part + skip_v[0:1, lanes] * x
                gated = ssd * silu(z_v[here, lanes].astype(jnp.float32))
                z_v[here, lanes] = (gated * gain_ref[:, lanes]).astype(jnp.bfloat16)
                total = total + gated * gated
        sq_v[here, :] = total

    def product(block, t):
        columns = pl.ds(pl.multiple_of(t * TILE, TILE), TILE)
        here = pl.ds(pl.multiple_of(block * own_rows, own_rows), own_rows)
        return jnp.dot(z_v[here, :], w_v[:, columns], preferred_element_type=jnp.float32)

    def sq_copy(s):
        target = lax.rem(head + s, n_head)
        here = pl.ds(pl.multiple_of(target * own_rows, own_rows), own_rows)
        return remote(sq_v.at[here], sq_in.at[s - 1], sq_send.at[s - 1], sq_recv.at[s - 1], head=target)

    def finish(slots):
        here = pl.ds(pl.multiple_of(head * own_rows, own_rows), own_rows)
        squares = sq_v[here, :]
        for s in range(1, n_head):
            sq_copy(s).wait_recv()
            squares = squares + sq_in[s - 1]
        scale = lax.rsqrt(jnp.sum(squares, axis=1, keepdims=True) / INNER + NORM_EPS)
        sq_v[here, :] = jnp.broadcast_to(scale, (own_rows, LANES))

        def last(t, _):
            total = product(head, t)
            for slot in range(slots):
                fin_copy(slot, t).wait_recv()
                total = total + recv_v[slot, t].astype(jnp.float32)
            columns = pl.ds(pl.multiple_of(t * TILE, TILE), TILE)
            scale = sq_v[here, :][:, 0:1]
            out_ref[:, columns] = (total * scale).astype(jnp.bfloat16)
            return 0

        lax.fori_loop(0, tiles, last, 0)

    if n_head == 4:
        by_x = head + 1 - 2 * lax.rem(head, 2)
        by_y = lax.rem(head + 2, 4)
        far = 3 - head
        half = tiles // 2
        per_block = own_rows // CHUNK

        def gates(block):
            lax.fori_loop(0, per_block, lambda i, _: (gate(block * per_block + i), 0)[1], 0)

        def mid_copy(t, target):
            return remote(send_v.at[0, t], mid_v.at[t], out_send.at[0, t], mid_recv.at[t], head=target)

        def fin_copy(slot, t):
            return remote(
                send_v.at[slot + 1, t], recv_v.at[slot, t], out_send.at[slot + 1, t], fin_recv.at[slot, t],
                head=by_x if slot == 0 else by_y,
            )

        def first(i, _):
            send_v[0, i] = product(far, i).astype(jnp.bfloat16)
            mid_copy(i, by_x).start()
            send_v[0, i + half] = product(far, i + half).astype(jnp.bfloat16)
            mid_copy(i + half, by_y).start()
            return 0

        turn = per_block + seq * (chunks - per_block) // n_seq

        def in_order(i, _):
            @pl.when(i == turn)
            def _():
                serve()
                gates(far)
                loads[4].wait()
                lax.fori_loop(0, half, first, 0)

            j = i // per_block
            block = 2 * lax.rem(head // 2 + j + 1, 2) + lax.rem(lax.rem(head, 2) + 1 + j // 2, 2)
            within(block * per_block + lax.rem(i, per_block))
            return 0

        lax.fori_loop(0, chunks, in_order, 0)
        gates(by_x)
        gates(by_y)

        def plain(i, _):
            send_v[1, i] = product(by_x, i).astype(jnp.bfloat16)
            fin_copy(0, i).start()
            send_v[2, i + half] = product(by_y, i + half).astype(jnp.bfloat16)
            fin_copy(1, i + half).start()
            return 0

        lax.fori_loop(0, half, plain, 0)
        gates(head)
        for s in range(1, n_head):
            sq_copy(s).start()

        def relayed(i, _):
            mine = product(by_x, i + half)
            mid_copy(i + half, by_y).wait_recv()
            send_v[1, i + half] = (mine + mid_v[i + half].astype(jnp.float32)).astype(jnp.bfloat16)
            fin_copy(0, i + half).start()
            mine = product(by_y, i)
            mid_copy(i, by_x).wait_recv()
            send_v[2, i] = (mine + mid_v[i].astype(jnp.float32)).astype(jnp.bfloat16)
            fin_copy(1, i).start()
            return 0

        lax.fori_loop(0, half, relayed, 0)
        finish(2)

        def sent(t, _):
            fin_copy(0, t).wait_send()
            fin_copy(1, t).wait_send()
            mid_copy(t, by_x).wait_send()
            return 0

        lax.fori_loop(0, tiles, sent, 0)
    else:
        def fin_copy(slot, t):
            return remote(
                send_v.at[slot, t], recv_v.at[slot, t], out_send.at[slot, t], fin_recv.at[slot, t],
                head=lax.rem(head + slot + 1, n_head),
            )

        def in_order(c, _):
            @pl.when(c == seq * chunks // n_seq)
            def _():
                serve()

            within(c)
            return 0

        lax.fori_loop(0, chunks, in_order, 0)
        lax.fori_loop(0, chunks, lambda c, _: (gate(c), 0)[1], 0)
        loads[4].wait()
        for s in range(1, n_head):
            sq_copy(s).start()

        def each(slot, _):
            def tile(t, _):
                send_v[slot, t] = product(lax.rem(head + slot + 1, n_head), t).astype(jnp.bfloat16)
                fin_copy(slot, t).start()
                return 0

            return lax.fori_loop(0, tiles, tile, 0)

        lax.fori_loop(0, n_head - 1, each, 0)
        finish(n_head - 1)

        def sent(slot, _):
            def tile(t, _):
                fin_copy(slot, t).wait_send()
                return 0

            return lax.fori_loop(0, tiles, tile, 0)

        lax.fori_loop(0, n_head - 1, sent, 0)

    for s in range(1, n_head):
        sq_copy(s).wait_send()

    @pl.when(seq < n_seq - 1)
    def _():
        for copy in rims:
            copy.wait_send()
        for k in range(pieces):
            carry_copy(k).wait_send()


def local(n_seq, n_head, x_in, z_gate, b_in, c_in, dt_raw, a_log, d_skip, conv_x, conv_bc, norm_gain, w_out):
    rows, chans = x_in.shape
    state = b_in.shape[1]
    width = w_out.shape[1]
    own = rows // n_head
    tiles = width // TILE
    chunks = rows // CHUNK
    pieces = min(8, chans // LANES)
    heads = a_log.shape[0]
    sends, mids, slots = (3, tiles, 2) if n_head == 4 else (n_head - 1, 1, n_head - 1)
    bf, f32 = jnp.bfloat16, jnp.float32
    any_spec = pl.BlockSpec(memory_space=pl.ANY)
    vmem = pl.BlockSpec(memory_space=pltpu.VMEM)
    dma = pltpu.SemaphoreType.DMA
    flops = 2 * rows * chans * (width + 3 * state)
    return pl.pallas_call(
        functools.partial(kernel, n_seq, n_head),
        out_shape=jax.ShapeDtypeStruct((own, width), bf),
        in_specs=[any_spec] * 5 + [vmem] * 6,
        out_specs=vmem,
        scratch_shapes=[
            pltpu.VMEM((RIM + rows, chans), bf),
            pltpu.VMEM((rows, chans), bf),
            pltpu.VMEM((chans, width), bf),
            pltpu.VMEM((RIM + rows, 2 * state), bf),
            pltpu.VMEM((rows, chans), f32),
            pltpu.VMEM((chunks * state, chans), bf),
            pltpu.VMEM((state, chans), f32),
            pltpu.VMEM((state, chans), bf),
            pltpu.VMEM((state, chans), bf),
            pltpu.VMEM((8 + CHUNK, chans), f32),
            pltpu.VMEM((8 + CHUNK, 2 * state), f32),
            pltpu.VMEM((rows, LANES), f32),
            pltpu.VMEM((LANES, LANES), f32),
            pltpu.VMEM((8, chans), f32),
            pltpu.VMEM((chunks * heads, CHUNK), f32),
            pltpu.VMEM((chunks * heads, CHUNK), f32),
            pltpu.VMEM((chunks * 8, chans), f32),
            pltpu.VMEM((8, chans), f32),
            pltpu.VMEM((rows, LANES), f32),
            pltpu.VMEM((n_head - 1, own, LANES), f32),
            pltpu.VMEM((sends, tiles, own, TILE), bf),
            pltpu.VMEM((mids, own, TILE), bf),
            pltpu.VMEM((slots, tiles, own, TILE), bf),
            dma((5,)), dma((3,)), dma((3,)), dma((pieces,)), dma((pieces,)),
            dma((n_head - 1,)), dma((n_head - 1,)),
            dma((sends, tiles)), dma((mids,)), dma((slots, tiles)),
        ],
        compiler_params=pltpu.CompilerParams(
            collective_id=0, has_side_effects=True, vmem_limit_bytes=62 * 1024 * 1024
        ),
        cost_estimate=pl.CostEstimate(
            flops=flops, bytes_accessed=2 * (2 * rows * chans + chans * width), transcendentals=rows * chans
        ),
    )(x_in, z_gate, b_in, c_in, w_out, dt_raw.T, a_log[None, :], d_skip[None, :], conv_x, conv_bc, norm_gain[None, :])


def solution(mesh):
    in_specs = (
        P("seq", "head"), P("seq", "head"), P("seq", None), P("seq", None), P("seq", "head"),
        P("head"), P("head"), P(None, "head"), P(), P("head"), P("head", None),
    )
    body = functools.partial(local, mesh.shape["seq"], mesh.shape["head"])
    return jax.shard_map(
        body, mesh=mesh, in_specs=in_specs, out_specs=P(("seq", "head"), None), check_vma=False
    )
```
